512 devices in a mesh: leaf: 8 (over z), wide: 64 (over y, x, core).
Axes of the slice: x: 4, y: 8, z: 8, core: 2. Of those that a mesh axis runs over, the one named last changes fastest.
Arguments:
- models: bfloat16 [64, 8, 256, 1024], P('wide', 'leaf'), may hold values from -6 to 6
- leaf_slot: int32 [64, 8], P('wide'), may hold values from 0 to 7, each once within a row
- diag_blocks: bfloat16 [64, 8, 1024, 1024], P('wide', 'leaf'), may hold values from -0.1875 to 0.1875
- leaf_in: bfloat16 [64, 8, 1024, 128], P('wide', 'leaf'), may hold values from -0.1875 to 0.1875
- leaf_out: bfloat16 [64, 8, 128, 1024], P('wide', 'leaf'), may hold values from -0.25 to 0.25
- leaf_up: bfloat16 [64, 8, 128, 128], P('wide', 'leaf'), may hold values from -0.1875 to 0.1875
- leaf_down: bfloat16 [64, 8, 128, 128], P('wide', 'leaf'), may hold values from -0.5 to 0.5
- leaf_couple: bfloat16 [64, 8, 8, 128, 128], P('wide', 'leaf'), may hold values from -0.1875 to 0.1875
- upper_up: bfloat16 [64, 2, 128, 128], P('wide'), as said below
- upper_down: bfloat16 [64, 2, 128, 128], P('wide'), as said below
- upper_couple: bfloat16 [64, 3, 4, 128, 128], P('wide'), as said below
Outputs:
- response: float32 [64, 8, 256, 1024], P('wide', 'leaf')
The draws below stay inside these ranges and needn't reach their ends.
Inputs may be any that keep to these rules, and one draw needn't show every extreme that they name: Each row of leaf_slot is a permutation; device j of group w holds the leaf at tree position w * 8 + leaf_slot[w, j]. `upper_up`: entries at w and v of level l agree whenever w // 4**l == v // 4**l. `upper_down`: entries at w and v of level l agree whenever w // 4**l == v // 4**l. `upper_couple`: entries at w and v of level l agree whenever w // 4**l == v // 4**l.
All inputs are finite; a program needn't handle non-finite values.
Results may differ from the reference program's by a relative error of at most 0.012.
Values may be sent and summed in bfloat16 or wider, within the bound.
No kernel may reach another device: no remote copies, remote signals or barrier semaphores. Data moves between devices by JAX's collectives and lax.ppermute only.
A program may use at most 64 MiB of HBM per device.

```python
import jax
import jax.numpy as jnp
from jax import lax

LEAF = 1024
RANK = 128
MODELS = 256
LEVELS = 3
N_LEAF = 8
N_WIDE = 64


def replicate(raw, count):
    wide = jnp.arange(N_WIDE)
    return jnp.stack([raw[wide // 4 ** level * 4 ** level, level] for level in range(count)], axis=1)


def draw_upper_up(key, part):
    key = jax.random.fold_in(key, 11)
    shape = (N_WIDE, LEVELS - 1, RANK, RANK)
    scale = (4.0 * RANK) ** (-0.5)
    raw = jax.random.normal(key, shape, jnp.float32) * scale
    return replicate(raw, LEVELS - 1).astype(jnp.bfloat16)


def draw_upper_down(key, part):
    key = jax.random.fold_in(key, 23)
    shape = (N_WIDE, LEVELS - 1, RANK, RANK)
    scale = (1.0 * RANK) ** (-0.5)
    raw = jax.random.normal(key, shape, jnp.float32) * scale
    return replicate(raw, LEVELS - 1).astype(jnp.bfloat16)


def draw_upper_couple(key, part):
    key = jax.random.fold_in(key, 37)
    shape = (N_WIDE, LEVELS, 4, RANK, RANK)
    scale = (3.0 * RANK) ** (-0.5)
    raw = jax.random.normal(key, shape, jnp.float32) * scale
    return replicate(raw, LEVELS).astype(jnp.bfloat16)


def steps_of(key, dims, cuts, low, largest):
    def one(dim, parts):
        draws = jax.random.uniform(jax.random.fold_in(jax.random.fold_in(key, 6), dim), (parts,), jnp.float32, low / len(cuts), largest / len(cuts))
        return jnp.repeat(jnp.exp(draws), dims[dim] // parts).reshape((-1,) + (1,) * (len(dims) - dim - 1))

    factor_of = one(*cuts[0])
    for cut in cuts[1:]:
        factor_of = factor_of * one(*cut)
    return factor_of


def gaussian(key, dims, deviation, reach, split=(), held_as=jnp.bfloat16):
    values = deviation * jax.random.normal(key, dims, jnp.float32)
    if split:
        values = values * steps_of(key, dims, split, -0.22, 0.18)
    return jnp.clip(values, -reach, reach).astype(held_as)


def setup_inputs(seed: int = 0) -> dict:
    key_list = jax.random.split(jax.random.key(seed), 12)
    return {
        "models": gaussian(key_list[0], (N_WIDE, N_LEAF, MODELS, LEAF), 1.0, 6.0, ((0, 64), (1, 8))),
        "leaf_slot": jax.vmap(lambda own: jax.random.permutation(own, N_LEAF))(jax.random.split(key_list[1], N_WIDE)).reshape((N_WIDE, N_LEAF)).astype(jnp.int32),
        "diag_blocks": gaussian(key_list[2], (N_WIDE, N_LEAF, LEAF, LEAF), LEAF ** -0.5, 0.1875, ((0, 64), (1, 8))),
        "leaf_in": gaussian(key_list[3], (N_WIDE, N_LEAF, LEAF, RANK), LEAF ** -0.5, 0.1875, ((0, 64), (1, 8))),
        "leaf_out": gaussian(key_list[4], (N_WIDE, N_LEAF, RANK, LEAF), ((LEVELS + 1) * RANK) ** -0.5, 0.25, ((0, 64), (1, 8))),
        "leaf_up": gaussian(key_list[5], (N_WIDE, N_LEAF, RANK, RANK), (N_LEAF * RANK) ** -0.5, 0.1875, ((0, 64), (1, 8))),
        "leaf_down": gaussian(key_list[6], (N_WIDE, N_LEAF, RANK, RANK), RANK ** -0.5, 0.5, ((0, 64), (1, 8))),
        "leaf_couple": gaussian(key_list[7], (N_WIDE, N_LEAF, N_LEAF, RANK, RANK), ((N_LEAF - 1) * RANK) ** -0.5, 0.1875, ((0, 64), (1, 8))),
        "upper_up": draw_upper_up(jax.random.fold_in(key_list[11], 71), 0),
        "upper_down": draw_upper_down(jax.random.fold_in(key_list[11], 71), 0),
        "upper_couple": draw_upper_couple(jax.random.fold_in(key_list[11], 71), 0),
    }


def round_trip(value):
    return lax.optimization_barrier(value.astype(jnp.bfloat16)).astype(jnp.float32)


def reference(models, leaf_slot, diag_blocks, leaf_in, leaf_out, leaf_up, leaf_down, leaf_couple, upper_up, upper_down, upper_couple):
    def lift(group):
        inputs, basis, upward = group
        coeff = jnp.einsum("jml,jlr->jmr", inputs.astype(jnp.float32), basis.astype(jnp.float32))
        rounded = round_trip(coeff)
        total = jnp.einsum("jmr,jrq->mq", rounded, upward.astype(jnp.float32))
        return rounded, total

    skeleton, current = lax.map(lift, (models, leaf_in, leaf_up))
    off_four = (1.0 - jnp.eye(4, dtype=jnp.float32))[None, :, :, None, None]
    nears = []
    for level in range(LEVELS):
        stride = 4 ** level
        nodes = N_WIDE // stride
        rounded = round_trip(current).reshape(nodes // 4, 4, MODELS, RANK)
        couple = upper_couple[::stride, level].astype(jnp.float32).reshape(nodes // 4, 4, 4, RANK, RANK) * off_four
        near = jnp.einsum("gsmr,gtsrq->gtmq", rounded, couple)
        nears.append(near.reshape(nodes, MODELS, RANK))
        if level + 1 < LEVELS:
            upward = upper_up[::stride, level].astype(jnp.float32).reshape(nodes // 4, 4, RANK, RANK)
            current = jnp.einsum("gsmr,gsrq->gmq", rounded, upward)
    field = nears[LEVELS - 1]
    for level in range(LEVELS - 2, -1, -1):
        stride = 4 ** level
        parent = jnp.repeat(round_trip(field), 4, axis=0)
        downward = upper_down[::stride, level].astype(jnp.float32)
        field = nears[level] + jnp.einsum("nmr,nrq->nmq", parent, downward)

    off_leaf = (1.0 - jnp.eye(N_LEAF, dtype=jnp.float32))[:, :, None, None]

    def finish(group):
        inputs, slots, blocks, outward, downward, couple, rounded, far = group
        chosen = jnp.take(couple, slots, axis=1).astype(jnp.float32) * off_leaf
        near = jnp.einsum("kmr,jkrq->jmq", rounded, chosen)
        total = near + jnp.einsum("mr,jrq->jmq", round_trip(far), downward.astype(jnp.float32))
        dense = jnp.einsum("jml,jlk->jmk", inputs.astype(jnp.float32), blocks.astype(jnp.float32))
        return dense + jnp.einsum("jmr,jrl->jml", round_trip(total), outward.astype(jnp.float32))

    return lax.map(finish, (models, leaf_slot, diag_blocks, leaf_out, leaf_down, leaf_couple, skeleton, field))
```

```python
import jax
import jax.numpy as jnp
from jax import lax
from jax.experimental import pallas as pl
from jax.experimental.pallas import tpu as pltpu
from jax.sharding import PartitionSpec as P

BF = jnp.bfloat16
F32 = jnp.float32


def mm(a, b):
    return jnp.dot(a, b, preferred_element_type=F32)


def call(body, shapes, scalars, arrays, params=(), flops=10**6, grant=32, name=None):
    n_scalars, n_arrays, n_params, n_out = len(scalars), len(arrays), len(params), len(shapes)

    def kernel(*refs):
        inside = n_scalars + n_arrays
        held = refs[inside + n_params + n_out : inside + 2 * n_params + n_out]
        copies = []
        for k in range(n_params):
            copy = pltpu.make_async_copy(refs[inside + k], held[k], refs[-1].at[k])
            copy.start()
            copies.append(copy)

        def fetch(k):
            def get():
                copies[k].wait()
                return held[k]

            return get

        outs = refs[inside + n_params : inside + n_params + n_out]
        body(*refs[:inside], *[fetch(k) for k in range(n_params)], *outs)

    moved = sum(a.size * a.dtype.itemsize for a in (*arrays, *params))
    return pl.pallas_call(
        kernel,
        out_shape=[jax.ShapeDtypeStruct(s, t) for s, t in shapes],
        in_specs=[pl.BlockSpec(memory_space=pltpu.SMEM)] * n_scalars
        + [pl.BlockSpec(memory_space=pltpu.VMEM)] * n_arrays
        + [pl.BlockSpec(memory_space=pltpu.HBM)] * n_params,
        out_specs=[pl.BlockSpec(memory_space=pltpu.VMEM)] * n_out,
        scratch_shapes=[pltpu.VMEM(a.shape, a.dtype) for a in params]
        + [pltpu.SemaphoreType.DMA((max(n_params, 1),))],
        compiler_params=pltpu.CompilerParams(vmem_limit_bytes=grant * 2**20),
        cost_estimate=pl.CostEstimate(flops=flops, bytes_accessed=moved, transcendentals=0),
        name=name,
    )(*scalars, *arrays, *params)


def total_of(ref, start, count):
    total = ref[start].astype(F32)
    for k in range(1, count):
        total = total + ref[start + k].astype(F32)
    return total


def first_kernel(models, leaf_in, leaf_up, lifted_ref, skeleton_ref):
    skeleton = mm(models()[...], leaf_in()[...]).astype(BF)
    skeleton_ref[...] = skeleton
    lifted_ref[...] = mm(skeleton, leaf_up()[...]).astype(BF).reshape(lifted_ref.shape)


def hold_kernel(upper_up_ref, held_ref):
    held_ref[...] = upper_up_ref[...]


def up_kernel(wide_ref, parts_ref, up_ref, sent_ref):
    wide = wide_ref[0]
    own = total_of(parts_ref, 0, parts_ref.shape[0]).astype(BF)
    parent = mm(own, up_ref[0]).astype(BF)
    top = mm(parent, up_ref[1]).astype(BF)
    for k in range(sent_ref.shape[0]):
        sent_ref[k] = top
    for k in range(16):
        sent_ref[wide // 16 * 16 + k] = parent
    for k in range(4):
        sent_ref[wide // 4 * 4 + k] = own


def down_kernel(wide_ref, heard_ref, couple_ref, upper_down, far_ref):
    wide = wide_ref[0]
    sums = []
    for level in range(3):
        step = 4**level
        first = wide // (4 * step) * 4
        for s in range(4):
            block = total_of(heard_ref, (first + s) * step, step)
            block = jnp.where(first + s == wide // step, jnp.zeros_like(block), block)
            sums.append(block.astype(BF))
    down_ref = upper_down()

    def near(level):
        field = None
        for s in range(4):
            term = mm(sums[4 * level + s], couple_ref[level, s])
            field = term if field is None else field + term
        return field

    field = near(2)
    for level in (1, 0):
        field = near(level) + mm(field.astype(BF), down_ref[level])
    rounded = field.astype(BF)
    for k in range(far_ref.shape[0]):
        far_ref[k] = rounded


def pair_kernel(own_ref, next_ref, pair_ref):
    pair_ref[0] = own_ref[...]
    pair_ref[1] = next_ref[...]


def dense_kernel(models_ref, diag_ref, dense_ref):
    dense_ref[...] = mm(models_ref[...], diag_ref[...])


def local_kernel(
    leaf_ref,
    slot_ref,
    next_ref,
    five_ref,
    six_ref,
    two_ref,
    dense_ref,
    couple,
    leaf_down,
    leaf_out,
    base_ref,
    weight_ref,
):
    leaf = leaf_ref[0]
    couple_ref = couple()
    near = mm(next_ref[...], couple_ref[slot_ref[leaf ^ 1]])
    for step, pair_ref in ((5, five_ref), (6, six_ref), (2, two_ref)):
        for k in range(2):
            near = near + mm(pair_ref[k], couple_ref[slot_ref[leaf ^ step ^ k]])
    out = leaf_out()[...]
    base_ref[...] = dense_ref[...] + mm(near.astype(BF), out)
    weight_ref[...] = mm(leaf_down()[...], out).astype(BF)


def last_kernel(far_ref, base_ref, weight_ref, response_ref):
    m, r = far_ref.shape[0] * far_ref.shape[1], far_ref.shape[2]
    response_ref[...] = base_ref[...] + mm(far_ref[...].reshape(m, r), weight_ref[...])


def shards(
    models,
    leaf_slot,
    diag_blocks,
    leaf_in,
    leaf_out,
    leaf_up,
    leaf_down,
    leaf_couple,
    upper_up,
    upper_down,
    upper_couple,
):
    inputs = models[0, 0]
    m, length = inputs.shape
    r = leaf_in.shape[-1]
    n_leaf = lax.axis_size("leaf")
    n_wide = lax.axis_size("wide")
    cut = m // n_leaf
    wide = lax.axis_index("wide").astype(jnp.int32).reshape(1)
    leaf = lax.axis_index("leaf").astype(jnp.int32).reshape(1)


    def partner(x, step):
        return lax.ppermute(x, "leaf", [(k, k ^ step) for k in range(n_leaf)])

    lifted, skeleton = call(
        first_kernel,
        [((n_leaf, cut, r), BF), ((m, r), BF)],
        [],
        [],
        [inputs, leaf_in[0, 0], leaf_up[0, 0]],
        flops=2 * m * length * r,
        grant=58,
        name="first",
    )
    lifted, upper_up = lax.optimization_barrier((lifted, upper_up))
    parts = lax.all_to_all(lifted, "leaf", 0, 0, tiled=True)
    (ups,) = call(hold_kernel, [(upper_up.shape[1:], BF)], [], [upper_up[0]], name="hold")
    ups, skeleton = lax.optimization_barrier((ups, skeleton))
    following = partner(skeleton, 1)
    parts, following = lax.optimization_barrier((parts, following))
    (sent,) = call(
        up_kernel, [((n_wide, cut, r), BF)], [wide], [parts, ups], name="up"
    )
    sent, skeleton = lax.optimization_barrier((sent, skeleton))
    heard = lax.all_to_all(sent, "wide", 0, 0, tiled=True)
    (pair,) = call(pair_kernel, [((2, m, r), BF)], [], [skeleton, following], name="pair")
    two, six, five = [partner(pair, step) for step in (2, 6, 5)]
    (far,) = call(
        down_kernel,
        [((n_leaf, cut, r), BF)],
        [wide],
        [heard, upper_couple[0]],
        [upper_down[0]],
        name="down",
    )
    far = lax.all_to_all(far, "leaf", 0, 0, tiled=True)
    (dense,) = call(
        dense_kernel,
        [((m, length), F32)],
        [],
        [inputs, diag_blocks[0, 0]],
        flops=2 * m * length * length,
        name="dense",
    )
    base, weight = call(
        local_kernel,
        [((m, length), F32), ((r, length), BF)],
        [leaf, leaf_slot[0]],
        [following, five, six, two, dense],
        [leaf_couple[0, 0], leaf_down[0, 0], leaf_out[0, 0]],
        flops=2 * m * length * r,
        name="local",
    )
    (response,) = call(
        last_kernel,
        [((m, length), F32)],
        [],
        [far, base, weight],
        flops=2 * m * length * r,
        name="last",
    )
    return response[None, None]


def solution(mesh):
    placed = (
        P("wide", "leaf", None, None),
        P("wide", None),
        P("wide", "leaf", None, None),
        P("wide", "leaf", None, None),
        P("wide", "leaf", None, None),
        P("wide", "leaf", None, None),
        P("wide", "leaf", None, None),
        P("wide", "leaf", None, None, None),
        P("wide", None, None, None),
        P("wide", None, None, None),
        P("wide", None, None, None, None),
    )
    return jax.shard_map(
        shards, mesh=mesh, in_specs=placed, out_specs=P("wide", "leaf", None, None), check_vma=False
    )
```

```python
import jax
import jax.numpy as jnp
from jax import lax
from jax.experimental import pallas as pl
from jax.experimental.pallas import tpu as pltpu
from jax.sharding import PartitionSpec as P

BF = jnp.bfloat16
F32 = jnp.float32


def mm(a, b):
    return jnp.dot(a, b, preferred_element_type=F32)


def call(body, shapes, scalars, arrays, params=(), flops=10**6, grant=32, name=None):
    n_scalars, n_arrays, n_params, n_out = len(scalars), len(arrays), len(params), len(shapes)

    def kernel(*refs):
        inside = n_scalars + n_arrays
        held = refs[inside + n_params + n_out : inside + 2 * n_params + n_out]
        copies = []
        for k in range(n_params):
            copy = pltpu.make_async_copy(refs[inside + k], held[k], refs[-1].at[k])
            copy.start()
            copies.append(copy)

        def fetch(k):
            def get():
                copies[k].wait()
                return held[k]

            return get

        outs = refs[inside + n_params : inside + n_params + n_out]
        body(*refs[:inside], *[fetch(k) for k in range(n_params)], *outs)

    moved = sum(a.size * a.dtype.itemsize for a in (*arrays, *params))
    return pl.pallas_call(
        kernel,
        out_shape=[jax.ShapeDtypeStruct(s, t) for s, t in shapes],
        in_specs=[pl.BlockSpec(memory_space=pltpu.SMEM)] * n_scalars
        + [pl.BlockSpec(memory_space=pltpu.VMEM)] * n_arrays
        + [pl.BlockSpec(memory_space=pltpu.HBM)] * n_params,
        out_specs=[pl.BlockSpec(memory_space=pltpu.VMEM)] * n_out,
        scratch_shapes=[pltpu.VMEM(a.shape, a.dtype) for a in params]
        + [pltpu.SemaphoreType.DMA((max(n_params, 1),))],
        compiler_params=pltpu.CompilerParams(vmem_limit_bytes=grant * 2**20),
        cost_estimate=pl.CostEstimate(flops=flops, bytes_accessed=moved, transcendentals=0),
        name=name,
    )(*scalars, *arrays, *params)


def total_of(ref, start, count):
    total = ref[start].astype(F32)
    for k in range(1, count):
        total = total + ref[start + k].astype(F32)
    return total


def first_kernel(models, leaf_in, leaf_up, lifted_ref, skeleton_ref):
    skeleton = mm(models()[...], leaf_in()[...]).astype(BF)
    skeleton_ref[...] = skeleton
    lifted_ref[...] = mm(skeleton, leaf_up()[...]).astype(BF).reshape(lifted_ref.shape)


def hold_kernel(upper_up_ref, held_ref):
    held_ref[...] = upper_up_ref[...]


def up_kernel(wide_ref, parts_ref, up_ref, sent_ref):
    wide = wide_ref[0]
    own = total_of(parts_ref, 0, parts_ref.shape[0]).astype(BF)
    parent = mm(own, up_ref[0]).astype(BF)
    top = mm(parent, up_ref[1]).astype(BF)
    for k in range(sent_ref.shape[0]):
        sent_ref[k] = top
    for k in range(16):
        sent_ref[wide // 16 * 16 + k] = parent
    for k in range(4):
        sent_ref[wide // 4 * 4 + k] = own


def fold_kernel(couple_ref, upper_down, folded_ref):
    down_ref = upper_down()
    r = down_ref.shape[-1]
    flat = (4 * r, r)
    folded_ref[0] = couple_ref[0]
    top = mm(couple_ref[2].reshape(flat), down_ref[1]).astype(BF)
    folded_ref[2] = mm(top, down_ref[0]).astype(BF).reshape(4, r, r)
    folded_ref[1] = mm(couple_ref[1].reshape(flat), down_ref[0]).astype(BF).reshape(4, r, r)


def down_kernel(wide_ref, heard_ref, folded_ref, far_ref):
    wide = wide_ref[0]
    field = None
    for level in (2, 1, 0):
        step = 4**level
        first = wide // (4 * step) * 4
        for s in range(4):
            block = total_of(heard_ref, (first + s) * step, step)
            block = jnp.where(first + s == wide // step, jnp.zeros_like(block), block)
            term = mm(block.astype(BF), folded_ref[level, s])
            field = term if field is None else field + term
    rounded = field.astype(BF)
    for k in range(far_ref.shape[0]):
        far_ref[k] = rounded


def dense_kernel(models_ref, diag_ref, dense_ref):
    dense_ref[...] = mm(models_ref[...], diag_ref[...])


def local_kernel(
    leaf_ref,
    slot_ref,
    next_ref,
    five_ref,
    six_ref,
    two_ref,
    dense_ref,
    couple,
    leaf_down,
    leaf_out,
    base_ref,
    weight_ref,
):
    leaf = leaf_ref[0]
    couple_ref = couple()
    near = mm(next_ref[...], couple_ref[slot_ref[leaf ^ 1]])
    for step, pair_ref in ((5, five_ref), (6, six_ref), (2, two_ref)):
        for k in range(2):
            near = near + mm(pair_ref[k], couple_ref[slot_ref[leaf ^ step ^ k]])
    out = leaf_out()[...]
    base_ref[...] = dense_ref[...] + mm(near.astype(BF), out)
    weight_ref[...] = mm(leaf_down()[...], out).astype(BF)


def last_kernel(far_ref, base_ref, weight_ref, response_ref, held_ref, sems):
    m, r = far_ref.shape[0] * far_ref.shape[1], far_ref.shape[2]
    far = far_ref[...].reshape(m, r)
    pieces = sems.shape[0]
    size = m // pieces
    copies = []
    for k in range(pieces):
        rows = slice(k * size, (k + 1) * size)
        held_ref[rows] = base_ref[rows] + mm(far[rows], weight_ref[...])
        copy = pltpu.make_async_copy(held_ref.at[rows], response_ref.at[rows], sems.at[k])
        copy.start()
        copies.append(copy)
    for copy in copies:
        copy.wait()


def last_call(far, base, weight):
    m, length = base.shape
    return pl.pallas_call(
        last_kernel,
        out_shape=jax.ShapeDtypeStruct(base.shape, F32),
        in_specs=[pl.BlockSpec(memory_space=pltpu.VMEM)] * 3,
        out_specs=pl.BlockSpec(memory_space=pl.ANY),
        scratch_shapes=[pltpu.VMEM(base.shape, F32), pltpu.SemaphoreType.DMA((4,))],
        compiler_params=pltpu.CompilerParams(vmem_limit_bytes=32 * 2**20),
        cost_estimate=pl.CostEstimate(
            flops=2 * m * length * weight.shape[0], bytes_accessed=8 * m * length, transcendentals=0
        ),
        name="last",
    )(far, base, weight)


def shards(
    models,
    leaf_slot,
    diag_blocks,
    leaf_in,
    leaf_out,
    leaf_up,
    leaf_down,
    leaf_couple,
    upper_up,
    upper_down,
    upper_couple,
):
    inputs = models[0, 0]
    m, length = inputs.shape
    r = leaf_in.shape[-1]
    n_leaf = lax.axis_size("leaf")
    n_wide = lax.axis_size("wide")
    cut = m // n_leaf
    wide = lax.axis_index("wide").astype(jnp.int32).reshape(1)
    leaf = lax.axis_index("leaf").astype(jnp.int32).reshape(1)


    def partner(x, step):
        return lax.ppermute(x, "leaf", [(k, k ^ step) for k in range(n_leaf)])

    lifted, skeleton = call(
        first_kernel,
        [((n_leaf, cut, r), BF), ((m, r), BF)],
        [],
        [],
        [inputs, leaf_in[0, 0], leaf_up[0, 0]],
        flops=2 * m * length * r,
        grant=58,
        name="first",
    )
    lifted, upper_up = lax.optimization_barrier((lifted, upper_up))
    parts = lax.all_to_all(lifted, "leaf", 0, 0, tiled=True)
    (ups,) = call(hold_kernel, [(upper_up.shape[1:], BF)], [], [upper_up[0]], name="hold")
    ups, skeleton = lax.optimization_barrier((ups, skeleton))
    following = partner(skeleton, 1)
    parts, following = lax.optimization_barrier((parts, following))
    (sent,) = call(
        up_kernel, [((n_wide, cut, r), BF)], [wide], [parts, ups], name="up"
    )
    sent, skeleton, upper_down = lax.optimization_barrier((sent, skeleton, upper_down))
    heard = lax.all_to_all(sent, "wide", 0, 0, tiled=True)
    pair = jnp.stack([skeleton, following])
    two, six, five = [partner(pair, step) for step in (2, 6, 5)]
    (folded,) = call(
        fold_kernel,
        [(upper_couple.shape[1:], BF)],
        [],
        [upper_couple[0]],
        [upper_down[0]],
        flops=24 * r * r * r,
        name="fold",
    )
    (far,) = call(
        down_kernel, [((n_leaf, cut, r), BF)], [wide], [heard, folded], name="down"
    )
    far = lax.all_to_all(far, "leaf", 0, 0, tiled=True)
    (dense,) = call(
        dense_kernel,
        [((m, length), F32)],
        [],
        [inputs, diag_blocks[0, 0]],
        flops=2 * m * length * length,
        name="dense",
    )
    base, weight = call(
        local_kernel,
        [((m, length), F32), ((r, length), BF)],
        [leaf, leaf_slot[0]],
        [following, five, six, two, dense],
        [leaf_couple[0, 0], leaf_down[0, 0], leaf_out[0, 0]],
        flops=2 * m * length * r,
        name="local",
    )
    response = last_call(far, base, weight)
    return response[None, None]


def solution(mesh):
    placed = (
        P("wide", "leaf", None, None),
        P("wide", None),
        P("wide", "leaf", None, None),
        P("wide", "leaf", None, None),
        P("wide", "leaf", None, None),
        P("wide", "leaf", None, None),
        P("wide", "leaf", None, None),
        P("wide", "leaf", None, None, None),
        P("wide", None, None, None),
        P("wide", None, None, None),
        P("wide", None, None, None, None),
    )
    return jax.shard_map(
        shards, mesh=mesh, in_specs=placed, out_specs=P("wide", "leaf", None, None), check_vma=False
    )
```

```python
import jax
import jax.numpy as jnp
from jax import lax
from jax.experimental import pallas as pl
from jax.experimental.pallas import tpu as pltpu
from jax.sharding import PartitionSpec as P

BF = jnp.bfloat16
F32 = jnp.float32


def mm(a, b):
    return jnp.dot(a, b, preferred_element_type=F32)


def call(body, shapes, scalars, arrays, params=(), flops=10**6, grant=32, name=None):
    n_scalars, n_arrays, n_params, n_out = len(scalars), len(arrays), len(params), len(shapes)

    def kernel(*refs):
        inside = n_scalars + n_arrays
        held = refs[inside + n_params + n_out : inside + 2 * n_params + n_out]
        copies = []
        for k in range(n_params):
            copy = pltpu.make_async_copy(refs[inside + k], held[k], refs[-1].at[k])
            copy.start()
            copies.append(copy)

        def fetch(k):
            def get():
                copies[k].wait()
                return held[k]

            return get

        outs = refs[inside + n_params : inside + n_params + n_out]
        body(*refs[:inside], *[fetch(k) for k in range(n_params)], *outs)

    moved = sum(a.size * a.dtype.itemsize for a in (*arrays, *params))
    return pl.pallas_call(
        kernel,
        out_shape=[jax.ShapeDtypeStruct(s, t) for s, t in shapes],
        in_specs=[pl.BlockSpec(memory_space=pltpu.SMEM)] * n_scalars
        + [pl.BlockSpec(memory_space=pltpu.VMEM)] * n_arrays
        + [pl.BlockSpec(memory_space=pltpu.HBM)] * n_params,
        out_specs=[pl.BlockSpec(memory_space=pltpu.VMEM)] * n_out,
        scratch_shapes=[pltpu.VMEM(a.shape, a.dtype) for a in params]
        + [pltpu.SemaphoreType.DMA((max(n_params, 1),))],
        compiler_params=pltpu.CompilerParams(vmem_limit_bytes=grant * 2**20),
        cost_estimate=pl.CostEstimate(flops=flops, bytes_accessed=moved, transcendentals=0),
        name=name,
    )(*scalars, *arrays, *params)


def total_of(ref, start, count):
    total = ref[start].astype(F32)
    for k in range(1, count):
        total = total + ref[start + k].astype(F32)
    return total


def first_kernel(models, leaf_in, leaf_up, lifted_ref, skeleton_ref):
    skeleton = mm(models()[...], leaf_in()[...]).astype(BF)
    skeleton_ref[...] = skeleton
    lifted_ref[...] = mm(skeleton, leaf_up()[...]).astype(BF).reshape(lifted_ref.shape)


def hold_kernel(upper_up_ref, held_ref):
    held_ref[...] = upper_up_ref[...]


def up_kernel(wide_ref, parts_ref, up_ref, sent_ref):
    wide = wide_ref[0]
    own = total_of(parts_ref, 0, parts_ref.shape[0]).astype(BF)
    parent = mm(own, up_ref[0]).astype(BF)
    top = mm(parent, up_ref[1]).astype(BF)
    for k in range(sent_ref.shape[0]):
        sent_ref[k] = top
    for k in range(16):
        sent_ref[wide // 16 * 16 + k] = parent
    for k in range(4):
        sent_ref[wide // 4 * 4 + k] = own


def fold_kernel(couple_ref, upper_down, folded_ref):
    down_ref = upper_down()
    r = down_ref.shape[-1]
    flat = (4 * r, r)
    folded_ref[0] = couple_ref[0]
    top = mm(couple_ref[2].reshape(flat), down_ref[1]).astype(BF)
    folded_ref[2] = mm(top, down_ref[0]).astype(BF).reshape(4, r, r)
    folded_ref[1] = mm(couple_ref[1].reshape(flat), down_ref[0]).astype(BF).reshape(4, r, r)


def down_kernel(wide_ref, heard_ref, folded_ref, far_ref):
    wide = wide_ref[0]
    field = None
    for level in (2, 1, 0):
        step = 4**level
        first = wide // (4 * step) * 4
        for s in range(4):
            block = total_of(heard_ref, (first + s) * step, step)
            block = jnp.where(first + s == wide // step, jnp.zeros_like(block), block)
            term = mm(block.astype(BF), folded_ref[level, s])
            field = term if field is None else field + term
    rounded = field.astype(BF)
    for k in range(far_ref.shape[0]):
        far_ref[k] = rounded


def dense_kernel(models_ref, diag_ref, dense_ref):
    dense_ref[...] = mm(models_ref[...], diag_ref[...])


def local_kernel(
    leaf_ref,
    slot_ref,
    next_ref,
    five_ref,
    six_ref,
    two_ref,
    dense_ref,
    couple,
    leaf_down,
    leaf_out,
    base_ref,
    weight_ref,
):
    leaf = leaf_ref[0]
    couple_ref = couple()
    near = mm(next_ref[...], couple_ref[slot_ref[leaf ^ 1]])
    for step, pair_ref in ((5, five_ref), (6, six_ref), (2, two_ref)):
        for k in range(2):
            near = near + mm(pair_ref[k], couple_ref[slot_ref[leaf ^ step ^ k]])
    out = leaf_out()[...]
    base_ref[...] = dense_ref[...] + mm(near.astype(BF), out)
    weight_ref[...] = mm(leaf_down()[...], out).astype(BF)


def last_kernel(far_ref, base_ref, weight_ref, response_ref, held_ref, sems):
    m, r = far_ref.shape[0] * far_ref.shape[1], far_ref.shape[2]
    far = far_ref[...].reshape(m, r)
    pieces = sems.shape[0]
    size = m // pieces
    copies = []
    for k in range(pieces):
        rows = slice(k * size, (k + 1) * size)
        held_ref[rows] = base_ref[rows] + mm(far[rows], weight_ref[...])
        copy = pltpu.make_async_copy(held_ref.at[rows], response_ref.at[rows], sems.at[k])
        copy.start()
        copies.append(copy)
    for copy in copies:
        copy.wait()


def last_call(far, base, weight):
    m, length = base.shape
    return pl.pallas_call(
        last_kernel,
        out_shape=jax.ShapeDtypeStruct(base.shape, F32),
        in_specs=[pl.BlockSpec(memory_space=pltpu.VMEM)] * 3,
        out_specs=pl.BlockSpec(memory_space=pl.ANY),
        scratch_shapes=[pltpu.VMEM(base.shape, F32), pltpu.SemaphoreType.DMA((4,))],
        compiler_params=pltpu.CompilerParams(vmem_limit_bytes=32 * 2**20),
        cost_estimate=pl.CostEstimate(
            flops=2 * m * length * weight.shape[0], bytes_accessed=8 * m * length, transcendentals=0
        ),
        name="last",
    )(far, base, weight)


def shards(
    models,
    leaf_slot,
    diag_blocks,
    leaf_in,
    leaf_out,
    leaf_up,
    leaf_down,
    leaf_couple,
    upper_up,
    upper_down,
    upper_couple,
):
    inputs = models[0, 0]
    m, length = inputs.shape
    r = leaf_in.shape[-1]
    n_leaf = lax.axis_size("leaf")
    n_wide = lax.axis_size("wide")
    cut = m // n_leaf
    wide = lax.axis_index("wide").astype(jnp.int32).reshape(1)
    leaf = lax.axis_index("leaf").astype(jnp.int32).reshape(1)


    def partner(x, step):
        return lax.ppermute(x, "leaf", [(k, k ^ step) for k in range(n_leaf)])

    lifted, skeleton = call(
        first_kernel,
        [((n_leaf, cut, r), BF), ((m, r), BF)],
        [],
        [],
        [inputs, leaf_in[0, 0], leaf_up[0, 0]],
        flops=2 * m * length * r,
        grant=58,
        name="first",
    )
    lifted, upper_up, upper_down = lax.optimization_barrier((lifted, upper_up, upper_down))
    parts = lax.all_to_all(lifted, "leaf", 0, 0, tiled=True)
    (ups,) = call(hold_kernel, [(upper_up.shape[1:], BF)], [], [upper_up[0]], name="hold")
    (folded,) = call(
        fold_kernel,
        [(upper_couple.shape[1:], BF)],
        [],
        [upper_couple[0]],
        [upper_down[0]],
        flops=24 * r * r * r,
        name="fold",
    )
    ups, folded, skeleton = lax.optimization_barrier((ups, folded, skeleton))
    following = partner(skeleton, 1)
    (sent,) = call(
        up_kernel, [((n_wide, cut, r), BF)], [wide], [parts, ups], name="up"
    )
    sent, skeleton = lax.optimization_barrier((sent, skeleton))
    heard = lax.all_to_all(sent, "wide", 0, 0, tiled=True)
    pair = jnp.stack([skeleton, following])
    two, six, five = [partner(pair, step) for step in (2, 6, 5)]
    (far,) = call(
        down_kernel, [((n_leaf, cut, r), BF)], [wide], [heard, folded], name="down"
    )
    far = lax.all_to_all(far, "leaf", 0, 0, tiled=True)
    (dense,) = call(
        dense_kernel,
        [((m, length), F32)],
        [],
        [inputs, diag_blocks[0, 0]],
        flops=2 * m * length * length,
        name="dense",
    )
    base, weight = call(
        local_kernel,
        [((m, length), F32), ((r, length), BF)],
        [leaf, leaf_slot[0]],
        [following, five, six, two, dense],
        [leaf_couple[0, 0], leaf_down[0, 0], leaf_out[0, 0]],
        flops=2 * m * length * r,
        name="local",
    )
    response = last_call(far, base, weight)
    return response[None, None]


def solution(mesh):
    placed = (
        P("wide", "leaf", None, None),
        P("wide", None),
        P("wide", "leaf", None, None),
        P("wide", "leaf", None, None),
        P("wide", "leaf", None, None),
        P("wide", "leaf", None, None),
        P("wide", "leaf", None, None),
        P("wide", "leaf", None, None, None),
        P("wide", None, None, None),
        P("wide", None, None, None),
        P("wide", None, None, None, None),
    )
    return jax.shard_map(
        shards, mesh=mesh, in_specs=placed, out_specs=P("wide", "leaf", None, None), check_vma=False
    )
```

```python
import jax
import jax.numpy as jnp
from jax import lax
from jax.experimental import pallas as pl
from jax.experimental.pallas import tpu as pltpu
from jax.sharding import PartitionSpec as P

BF = jnp.bfloat16
F32 = jnp.float32


def mm(a, b):
    return jnp.dot(a, b, preferred_element_type=F32)


def call(body, shapes, scalars, arrays, params=(), flops=10**6, grant=32, name=None):
    n_scalars, n_arrays, n_params, n_out = len(scalars), len(arrays), len(params), len(shapes)

    def kernel(*refs):
        inside = n_scalars + n_arrays
        held = refs[inside + n_params + n_out : inside + 2 * n_params + n_out]
        copies = []
        for k in range(n_params):
            copy = pltpu.make_async_copy(refs[inside + k], held[k], refs[-1].at[k])
            copy.start()
            copies.append(copy)

        def fetch(k):
            def get():
                copies[k].wait()
                return held[k]

            return get

        outs = refs[inside + n_params : inside + n_params + n_out]
        body(*refs[:inside], *[fetch(k) for k in range(n_params)], *outs)

    moved = sum(a.size * a.dtype.itemsize for a in (*arrays, *params))
    return pl.pallas_call(
        kernel,
        out_shape=[jax.ShapeDtypeStruct(s, t) for s, t in shapes],
        in_specs=[pl.BlockSpec(memory_space=pltpu.SMEM)] * n_scalars
        + [pl.BlockSpec(memory_space=pltpu.VMEM)] * n_arrays
        + [pl.BlockSpec(memory_space=pltpu.HBM)] * n_params,
        out_specs=[pl.BlockSpec(memory_space=pltpu.VMEM)] * n_out,
        scratch_shapes=[pltpu.VMEM(a.shape, a.dtype) for a in params]
        + [pltpu.SemaphoreType.DMA((max(n_params, 1),))],
        compiler_params=pltpu.CompilerParams(vmem_limit_bytes=grant * 2**20),
        cost_estimate=pl.CostEstimate(flops=flops, bytes_accessed=moved, transcendentals=0),
        name=name,
    )(*scalars, *arrays, *params)


def total_of(ref, start, count):
    total = ref[start].astype(F32)
    for k in range(1, count):
        total = total + ref[start + k].astype(F32)
    return total


def first_kernel(models_ref, in_ref, up_ref, lifted_ref, skeleton_ref, models, leaf_in, up, sems):
    half = models.shape[1] // 2
    copies = []
    for k in range(2):
        cut = pl.ds(k * half, half)
        copies.append(
            pltpu.make_async_copy(models_ref.at[:, cut], models.at[:, cut], sems.at[2 * k])
        )
        copies.append(pltpu.make_async_copy(in_ref.at[cut], leaf_in.at[cut], sems.at[2 * k + 1]))
    copies.append(pltpu.make_async_copy(up_ref, up, sems.at[4]))
    for copy in copies:
        copy.start()
    coeff = None
    for k in range(2):
        cut = pl.ds(k * half, half)
        copies[2 * k].wait()
        copies[2 * k + 1].wait()
        term = mm(models[:, cut], leaf_in[cut])
        coeff = term if coeff is None else coeff + term
    skeleton = coeff.astype(BF)
    skeleton_ref[...] = skeleton
    copies[4].wait()
    lifted_ref[...] = mm(skeleton, up[...]).astype(BF).reshape(lifted_ref.shape)


def first_call(models, leaf_in, leaf_up, n_leaf):
    m, length = models.shape
    r = leaf_in.shape[1]
    return pl.pallas_call(
        first_kernel,
        out_shape=[
            jax.ShapeDtypeStruct((n_leaf, m // n_leaf, r), BF),
            jax.ShapeDtypeStruct((m, r), BF),
        ],
        in_specs=[pl.BlockSpec(memory_space=pl.ANY)] * 3,
        out_specs=[pl.BlockSpec(memory_space=pltpu.VMEM)] * 2,
        scratch_shapes=[pltpu.VMEM(a.shape, BF) for a in (models, leaf_in, leaf_up)]
        + [pltpu.SemaphoreType.DMA((5,))],
        compiler_params=pltpu.CompilerParams(vmem_limit_bytes=58 * 2**20),
        cost_estimate=pl.CostEstimate(
            flops=2 * m * length * r, bytes_accessed=2 * m * length, transcendentals=0
        ),
        name="first",
    )(models, leaf_in, leaf_up)


def step_kernel(leaf_ref, same_ref):
    same_ref[0] = leaf_ref[0]


def step_call(leaf):
    return pl.pallas_call(
        step_kernel,
        out_shape=jax.ShapeDtypeStruct(leaf.shape, leaf.dtype),
        in_specs=[pl.BlockSpec(memory_space=pltpu.SMEM)],
        out_specs=pl.BlockSpec(memory_space=pltpu.SMEM),
        name="step",
    )(leaf)


def hold_kernel(upper_up_ref, held_ref):
    held_ref[...] = upper_up_ref[...]


def up_kernel(wide_ref, parts_ref, up_ref, sent_ref):
    wide = wide_ref[0]
    own = total_of(parts_ref, 0, parts_ref.shape[0]).astype(BF)
    parent = mm(own, up_ref[0]).astype(BF)
    top = mm(parent, up_ref[1]).astype(BF)
    for k in range(sent_ref.shape[0]):
        sent_ref[k] = top
    for k in range(16):
        sent_ref[wide // 16 * 16 + k] = parent
    for k in range(4):
        sent_ref[wide // 4 * 4 + k] = own


def fold_kernel(couple_ref, upper_down, folded_ref):
    down_ref = upper_down()
    r = down_ref.shape[-1]
    flat = (4 * r, r)
    folded_ref[0] = couple_ref[0]
    top = mm(couple_ref[2].reshape(flat), down_ref[1]).astype(BF)
    folded_ref[2] = mm(top, down_ref[0]).astype(BF).reshape(4, r, r)
    folded_ref[1] = mm(couple_ref[1].reshape(flat), down_ref[0]).astype(BF).reshape(4, r, r)


def down_kernel(wide_ref, heard_ref, folded_ref, far_ref):
    wide = wide_ref[0]
    field = None
    for level in (2, 1, 0):
        step = 4**level
        first = wide // (4 * step) * 4
        for s in range(4):
            block = total_of(heard_ref, (first + s) * step, step)
            block = jnp.where(first + s == wide // step, jnp.zeros_like(block), block)
            term = mm(block.astype(BF), folded_ref[level, s])
            field = term if field is None else field + term
    rounded = field.astype(BF)
    for k in range(far_ref.shape[0]):
        far_ref[k] = rounded


def dense_kernel(models_ref, diag_ref, dense_ref):
    dense_ref[...] = mm(models_ref[...], diag_ref[...])


def local_kernel(
    leaf_ref,
    slot_ref,
    next_ref,
    five_ref,
    six_ref,
    two_ref,
    dense_ref,
    couple,
    leaf_down,
    leaf_out,
    base_ref,
    weight_ref,
):
    leaf = leaf_ref[0]
    couple_ref = couple()
    near = mm(next_ref[...], couple_ref[slot_ref[leaf ^ 1]])
    for step, pair_ref in ((5, five_ref), (6, six_ref), (2, two_ref)):
        for k in range(2):
            near = near + mm(pair_ref[k], couple_ref[slot_ref[leaf ^ step ^ k]])
    out = leaf_out()[...]
    base_ref[...] = dense_ref[...] + mm(near.astype(BF), out)
    weight_ref[...] = mm(leaf_down()[...], out).astype(BF)


def last_kernel(far_ref, base_ref, weight_ref, response_ref, held_ref, sems):
    m, r = far_ref.shape[0] * far_ref.shape[1], far_ref.shape[2]
    far = far_ref[...].reshape(m, r)
    pieces = sems.shape[0]
    size = m // pieces
    copies = []
    for k in range(pieces):
        rows = slice(k * size, (k + 1) * size)
        held_ref[rows] = base_ref[rows] + mm(far[rows], weight_ref[...])
        copy = pltpu.make_async_copy(held_ref.at[rows], response_ref.at[rows], sems.at[k])
        copy.start()
        copies.append(copy)
    for copy in copies:
        copy.wait()


def last_call(far, base, weight):
    m, length = base.shape
    return pl.pallas_call(
        last_kernel,
        out_shape=jax.ShapeDtypeStruct(base.shape, F32),
        in_specs=[pl.BlockSpec(memory_space=pltpu.VMEM)] * 3,
        out_specs=pl.BlockSpec(memory_space=pl.ANY),
        scratch_shapes=[pltpu.VMEM(base.shape, F32), pltpu.SemaphoreType.DMA((4,))],
        compiler_params=pltpu.CompilerParams(vmem_limit_bytes=32 * 2**20),
        cost_estimate=pl.CostEstimate(
            flops=2 * m * length * weight.shape[0], bytes_accessed=8 * m * length, transcendentals=0
        ),
        name="last",
    )(far, base, weight)


def shards(
    models,
    leaf_slot,
    diag_blocks,
    leaf_in,
    leaf_out,
    leaf_up,
    leaf_down,
    leaf_couple,
    upper_up,
    upper_down,
    upper_couple,
):
    inputs = models[0, 0]
    m, length = inputs.shape
    r = leaf_in.shape[-1]
    n_leaf = lax.axis_size("leaf")
    n_wide = lax.axis_size("wide")
    cut = m // n_leaf
    wide = lax.axis_index("wide").astype(jnp.int32).reshape(1)
    leaf = lax.axis_index("leaf").astype(jnp.int32).reshape(1)


    def partner(x, step):
        return lax.ppermute(x, "leaf", [(k, k ^ step) for k in range(n_leaf)])

    lifted, skeleton = first_call(inputs, leaf_in[0, 0], leaf_up[0, 0], n_leaf)
    lifted, upper_up, leaf = lax.optimization_barrier((lifted, upper_up, leaf))
    parts = lax.all_to_all(lifted, "leaf", 0, 0, tiled=True)
    leaf, skeleton = lax.optimization_barrier((step_call(leaf), skeleton))
    following = partner(skeleton, 1)
    (ups,) = call(hold_kernel, [(upper_up.shape[1:], BF)], [], [upper_up[0]], name="hold")
    (sent,) = call(
        up_kernel, [((n_wide, cut, r), BF)], [wide], [parts, ups], name="up"
    )
    sent, skeleton, following, upper_down = lax.optimization_barrier(
        (sent, skeleton, following, upper_down)
    )
    heard = lax.all_to_all(sent, "wide", 0, 0, tiled=True)
    pair = jnp.stack([skeleton, following])
    two, six, five = [partner(pair, step) for step in (2, 6, 5)]
    (folded,) = call(
        fold_kernel,
        [(upper_couple.shape[1:], BF)],
        [],
        [upper_couple[0]],
        [upper_down[0]],
        flops=24 * r * r * r,
        name="fold",
    )
    (far,) = call(
        down_kernel, [((n_leaf, cut, r), BF)], [wide], [heard, folded], name="down"
    )
    far = lax.all_to_all(far, "leaf", 0, 0, tiled=True)
    (dense,) = call(
        dense_kernel,
        [((m, length), F32)],
        [],
        [inputs, diag_blocks[0, 0]],
        flops=2 * m * length * length,
        name="dense",
    )
    base, weight = call(
        local_kernel,
        [((m, length), F32), ((r, length), BF)],
        [leaf, leaf_slot[0]],
        [following, five, six, two, dense],
        [leaf_couple[0, 0], leaf_down[0, 0], leaf_out[0, 0]],
        flops=2 * m * length * r,
        name="local",
    )
    response = last_call(far, base, weight)
    return response[None, None]


def solution(mesh):
    placed = (
        P("wide", "leaf", None, None),
        P("wide", None),
        P("wide", "leaf", None, None),
        P("wide", "leaf", None, None),
        P("wide", "leaf", None, None),
        P("wide", "leaf", None, None),
        P("wide", "leaf", None, None),
        P("wide", "leaf", None, None, None),
        P("wide", None, None, None),
        P("wide", None, None, None),
        P("wide", None, None, None, None),
    )
    return jax.shard_map(
        shards, mesh=mesh, in_specs=placed, out_specs=P("wide", "leaf", None, None), check_vma=False
    )
```

```python
import jax
import jax.numpy as jnp
from jax import lax
from jax.experimental import pallas as pl
from jax.experimental.pallas import tpu as pltpu
from jax.sharding import PartitionSpec as P

BF = jnp.bfloat16
F32 = jnp.float32


def mm(a, b):
    return jnp.dot(a, b, preferred_element_type=F32)


def call(body, shapes, scalars, arrays, params=(), flops=10**6, grant=32, name=None):
    n_scalars, n_arrays, n_params, n_out = len(scalars), len(arrays), len(params), len(shapes)

    def kernel(*refs):
        inside = n_scalars + n_arrays
        held = refs[inside + n_params + n_out : inside + 2 * n_params + n_out]
        copies = []
        for k in range(n_params):
            copy = pltpu.make_async_copy(refs[inside + k], held[k], refs[-1].at[k])
            copy.start()
            copies.append(copy)

        def fetch(k):
            def get():
                copies[k].wait()
                return held[k]

            return get

        outs = refs[inside + n_params : inside + n_params + n_out]
        body(*refs[:inside], *[fetch(k) for k in range(n_params)], *outs)

    moved = sum(a.size * a.dtype.itemsize for a in (*arrays, *params))
    return pl.pallas_call(
        kernel,
        out_shape=[jax.ShapeDtypeStruct(s, t) for s, t in shapes],
        in_specs=[pl.BlockSpec(memory_space=pltpu.SMEM)] * n_scalars
        + [pl.BlockSpec(memory_space=pltpu.VMEM)] * n_arrays
        + [pl.BlockSpec(memory_space=pltpu.HBM)] * n_params,
        out_specs=[pl.BlockSpec(memory_space=pltpu.VMEM)] * n_out,
        scratch_shapes=[pltpu.VMEM(a.shape, a.dtype) for a in params]
        + [pltpu.SemaphoreType.DMA((max(n_params, 1),))],
        compiler_params=pltpu.CompilerParams(vmem_limit_bytes=grant * 2**20),
        cost_estimate=pl.CostEstimate(flops=flops, bytes_accessed=moved, transcendentals=0),
        name=name,
    )(*scalars, *arrays, *params)


def total_of(ref, start, count):
    total = ref[start].astype(F32)
    for k in range(1, count):
        total = total + ref[start + k].astype(F32)
    return total


def first_kernel(
    models_ref, in_ref, up_ref, lifted_ref, skeleton_ref, pair_ref, models, leaf_in, up, sems
):
    half = models.shape[1] // 2
    copies = []
    for k in range(2):
        cut = pl.ds(k * half, half)
        copies.append(
            pltpu.make_async_copy(models_ref.at[:, cut], models.at[:, cut], sems.at[2 * k])
        )
        copies.append(pltpu.make_async_copy(in_ref.at[cut], leaf_in.at[cut], sems.at[2 * k + 1]))
    copies.append(pltpu.make_async_copy(up_ref, up, sems.at[4]))
    for copy in copies:
        copy.start()
    coeff = None
    for k in range(2):
        cut = pl.ds(k * half, half)
        copies[2 * k].wait()
        copies[2 * k + 1].wait()
        term = mm(models[:, cut], leaf_in[cut])
        coeff = term if coeff is None else coeff + term
    skeleton = coeff.astype(BF)
    skeleton_ref[...] = skeleton
    pair_ref[0] = skeleton
    pair_ref[1] = skeleton
    copies[4].wait()
    lifted_ref[...] = mm(skeleton, up[...]).astype(BF).reshape(lifted_ref.shape)


def first_call(models, leaf_in, leaf_up, n_leaf):
    m, length = models.shape
    r = leaf_in.shape[1]
    return pl.pallas_call(
        first_kernel,
        out_shape=[
            jax.ShapeDtypeStruct((n_leaf, m // n_leaf, r), BF),
            jax.ShapeDtypeStruct((m, r), BF),
            jax.ShapeDtypeStruct((2, m, r), BF),
        ],
        in_specs=[pl.BlockSpec(memory_space=pl.ANY)] * 3,
        out_specs=[pl.BlockSpec(memory_space=pltpu.VMEM)] * 3,
        scratch_shapes=[pltpu.VMEM(a.shape, BF) for a in (models, leaf_in, leaf_up)]
        + [pltpu.SemaphoreType.DMA((5,))],
        compiler_params=pltpu.CompilerParams(vmem_limit_bytes=58 * 2**20),
        cost_estimate=pl.CostEstimate(
            flops=2 * m * length * r, bytes_accessed=2 * m * length, transcendentals=0
        ),
        name="first",
    )(models, leaf_in, leaf_up)


def step_kernel(leaf_ref, same_ref):
    same_ref[0] = leaf_ref[0]


def step_call(leaf):
    return pl.pallas_call(
        step_kernel,
        out_shape=jax.ShapeDtypeStruct(leaf.shape, leaf.dtype),
        in_specs=[pl.BlockSpec(memory_space=pltpu.SMEM)],
        out_specs=pl.BlockSpec(memory_space=pltpu.SMEM),
        name="step",
    )(leaf)


def hold_kernel(weight_ref, held_ref):
    held_ref[...] = weight_ref[...]


def up_kernel(wide_ref, parts_ref, up_ref, sent_ref):
    wide = wide_ref[0]
    own = total_of(parts_ref, 0, parts_ref.shape[0]).astype(BF)
    parent = mm(own, up_ref[0]).astype(BF)
    top = mm(parent, up_ref[1]).astype(BF)
    for k in range(sent_ref.shape[0]):
        sent_ref[k] = top
    for k in range(16):
        sent_ref[wide // 16 * 16 + k] = parent
    for k in range(4):
        sent_ref[wide // 4 * 4 + k] = own


def down_kernel(wide_ref, heard_ref, couple_ref, down_ref, far_ref):
    wide = wide_ref[0]
    field = None
    for level in (2, 1, 0):
        if field is not None:
            field = mm(field.astype(BF), down_ref[level])
        step = 4**level
        first = wide // (4 * step) * 4
        for s in range(4):
            block = total_of(heard_ref, (first + s) * step, step)
            block = jnp.where(first + s == wide // step, jnp.zeros_like(block), block)
            term = mm(block.astype(BF), couple_ref[level, s])
            field = term if field is None else field + term
    rounded = field.astype(BF)
    for k in range(far_ref.shape[0]):
        far_ref[k] = rounded


def dense_kernel(models_ref, diag_ref, dense_ref):
    dense_ref[...] = mm(models_ref[...], diag_ref[...])


def local_kernel(
    leaf_ref,
    slot_ref,
    next_ref,
    five_ref,
    six_ref,
    two_ref,
    dense_ref,
    couple,
    leaf_down,
    leaf_out,
    base_ref,
    weight_ref,
):
    leaf = leaf_ref[0]
    couple_ref = couple()
    near = mm(next_ref[...], couple_ref[slot_ref[leaf ^ 1]])
    for step, pair_ref in ((5, five_ref), (6, six_ref), (2, two_ref)):
        for k in range(2):
            near = near + mm(pair_ref[k], couple_ref[slot_ref[leaf ^ step ^ k]])
    out = leaf_out()[...]
    base_ref[...] = dense_ref[...] + mm(near.astype(BF), out)
    weight_ref[...] = mm(leaf_down()[...], out).astype(BF)


def last_kernel(far_ref, base_ref, weight_ref, response_ref, held_ref, sems):
    m, r = far_ref.shape[0] * far_ref.shape[1], far_ref.shape[2]
    far = far_ref[...].reshape(m, r)
    pieces = sems.shape[0]
    size = m // pieces
    copies = []
    for k in range(pieces):
        rows = slice(k * size, (k + 1) * size)
        held_ref[rows] = base_ref[rows] + mm(far[rows], weight_ref[...])
        copy = pltpu.make_async_copy(held_ref.at[rows], response_ref.at[rows], sems.at[k])
        copy.start()
        copies.append(copy)
    for copy in copies:
        copy.wait()


def last_call(far, base, weight):
    m, length = base.shape
    return pl.pallas_call(
        last_kernel,
        out_shape=jax.ShapeDtypeStruct(base.shape, F32),
        in_specs=[pl.BlockSpec(memory_space=pltpu.VMEM)] * 3,
        out_specs=pl.BlockSpec(memory_space=pl.ANY),
        scratch_shapes=[pltpu.VMEM(base.shape, F32), pltpu.SemaphoreType.DMA((4,))],
        compiler_params=pltpu.CompilerParams(vmem_limit_bytes=32 * 2**20),
        cost_estimate=pl.CostEstimate(
            flops=2 * m * length * weight.shape[0], bytes_accessed=8 * m * length, transcendentals=0
        ),
        name="last",
    )(far, base, weight)


def shards(
    models,
    leaf_slot,
    diag_blocks,
    leaf_in,
    leaf_out,
    leaf_up,
    leaf_down,
    leaf_couple,
    upper_up,
    upper_down,
    upper_couple,
):
    inputs = models[0, 0]
    m, length = inputs.shape
    r = leaf_in.shape[-1]
    n_leaf = lax.axis_size("leaf")
    n_wide = lax.axis_size("wide")
    cut = m // n_leaf
    wide = lax.axis_index("wide").astype(jnp.int32).reshape(1)
    leaf = lax.axis_index("leaf").astype(jnp.int32).reshape(1)


    def partner(x, step):
        return lax.ppermute(x, "leaf", [(k, k ^ step) for k in range(n_leaf)])

    lifted, skeleton, pair = first_call(inputs, leaf_in[0, 0], leaf_up[0, 0], n_leaf)
    lifted, upper_up, leaf = lax.optimization_barrier((lifted, upper_up, leaf))
    parts = lax.all_to_all(lifted, "leaf", 0, 0, tiled=True)
    leaf, skeleton = lax.optimization_barrier((step_call(leaf), skeleton))
    following = partner(skeleton, 1)
    (ups,) = call(hold_kernel, [(upper_up.shape[1:], BF)], [], [upper_up[0]], name="hold")
    (sent,) = call(
        up_kernel, [((n_wide, cut, r), BF)], [wide], [parts, ups], name="up"
    )
    sent, following, upper_down = lax.optimization_barrier((sent, following, upper_down))
    heard = lax.all_to_all(sent, "wide", 0, 0, tiled=True)
    pair = lax.dynamic_update_slice(pair, following[None], (1, 0, 0))
    two, six, five = [partner(pair, step) for step in (2, 6, 5)]
    (downs,) = call(hold_kernel, [(upper_down.shape[1:], BF)], [], [upper_down[0]], name="hold_down")
    (far,) = call(
        down_kernel,
        [((n_leaf, cut, r), BF)],
        [wide],
        [heard, upper_couple[0], downs],
        name="down",
    )
    far = lax.all_to_all(far, "leaf", 0, 0, tiled=True)
    (dense,) = call(
        dense_kernel,
        [((m, length), F32)],
        [],
        [inputs, diag_blocks[0, 0]],
        flops=2 * m * length * length,
        name="dense",
    )
    base, weight = call(
        local_kernel,
        [((m, length), F32), ((r, length), BF)],
        [leaf, leaf_slot[0]],
        [following, five, six, two, dense],
        [leaf_couple[0, 0], leaf_down[0, 0], leaf_out[0, 0]],
        flops=2 * m * length * r,
        name="local",
    )
    response = last_call(far, base, weight)
    return response[None, None]


def solution(mesh):
    placed = (
        P("wide", "leaf", None, None),
        P("wide", None),
        P("wide", "leaf", None, None),
        P("wide", "leaf", None, None),
        P("wide", "leaf", None, None),
        P("wide", "leaf", None, None),
        P("wide", "leaf", None, None),
        P("wide", "leaf", None, None, None),
        P("wide", None, None, None),
        P("wide", None, None, None),
        P("wide", None, None, None, None),
    )
    return jax.shard_map(
        shards, mesh=mesh, in_specs=placed, out_specs=P("wide", "leaf", None, None), check_vma=False
    )
```

```python
import jax
import jax.numpy as jnp
from jax import lax
from jax.experimental import pallas as pl
from jax.experimental.pallas import tpu as pltpu
from jax.sharding import PartitionSpec as P

BF = jnp.bfloat16
F32 = jnp.float32


def mm(a, b):
    return jnp.dot(a, b, preferred_element_type=F32)


def call(body, shapes, scalars, arrays, params=(), flops=10**6, grant=32, name=None):
    n_scalars, n_arrays, n_params, n_out = len(scalars), len(arrays), len(params), len(shapes)

    def kernel(*refs):
        inside = n_scalars + n_arrays
        held = refs[inside + n_params + n_out : inside + 2 * n_params + n_out]
        copies = []
        for k in range(n_params):
            copy = pltpu.make_async_copy(refs[inside + k], held[k], refs[-1].at[k])
            copy.start()
            copies.append(copy)

        def fetch(k):
            def get():
                copies[k].wait()
                return held[k]

            return get

        outs = refs[inside + n_params : inside + n_params + n_out]
        body(*refs[:inside], *[fetch(k) for k in range(n_params)], *outs)

    moved = sum(a.size * a.dtype.itemsize for a in (*arrays, *params))
    return pl.pallas_call(
        kernel,
        out_shape=[jax.ShapeDtypeStruct(s, t) for s, t in shapes],
        in_specs=[pl.BlockSpec(memory_space=pltpu.SMEM)] * n_scalars
        + [pl.BlockSpec(memory_space=pltpu.VMEM)] * n_arrays
        + [pl.BlockSpec(memory_space=pltpu.HBM)] * n_params,
        out_specs=[pl.BlockSpec(memory_space=pltpu.VMEM)] * n_out,
        scratch_shapes=[pltpu.VMEM(a.shape, a.dtype) for a in params]
        + [pltpu.SemaphoreType.DMA((max(n_params, 1),))],
        compiler_params=pltpu.CompilerParams(vmem_limit_bytes=grant * 2**20),
        cost_estimate=pl.CostEstimate(flops=flops, bytes_accessed=moved, transcendentals=0),
        name=name,
    )(*scalars, *arrays, *params)


def total_of(ref, start, count):
    total = ref[start].astype(F32)
    for k in range(1, count):
        total = total + ref[start + k].astype(F32)
    return total


def first_kernel(models_ref, in_ref, up_ref, lifted_ref, skeleton_ref, models, leaf_in, up, sems):
    half = models.shape[1] // 2
    copies = []
    for k in range(2):
        cut = pl.ds(k * half, half)
        copies.append(
            pltpu.make_async_copy(models_ref.at[:, cut], models.at[:, cut], sems.at[2 * k])
        )
        copies.append(pltpu.make_async_copy(in_ref.at[cut], leaf_in.at[cut], sems.at[2 * k + 1]))
    copies.append(pltpu.make_async_copy(up_ref, up, sems.at[4]))
    for copy in copies:
        copy.start()
    coeff = None
    for k in range(2):
        cut = pl.ds(k * half, half)
        copies[2 * k].wait()
        copies[2 * k + 1].wait()
        term = mm(models[:, cut], leaf_in[cut])
        coeff = term if coeff is None else coeff + term
    skeleton = coeff.astype(BF)
    skeleton_ref[...] = skeleton
    copies[4].wait()
    lifted_ref[...] = mm(skeleton, up[...]).astype(BF).reshape(lifted_ref.shape)


def first_call(models, leaf_in, leaf_up, n_leaf):
    m, length = models.shape
    r = leaf_in.shape[1]
    return pl.pallas_call(
        first_kernel,
        out_shape=[
            jax.ShapeDtypeStruct((n_leaf, m // n_leaf, r), BF),
            jax.ShapeDtypeStruct((m, r), BF),
        ],
        in_specs=[pl.BlockSpec(memory_space=pl.ANY)] * 3,
        out_specs=[pl.BlockSpec(memory_space=pltpu.VMEM)] * 2,
        scratch_shapes=[pltpu.VMEM(a.shape, BF) for a in (models, leaf_in, leaf_up)]
        + [pltpu.SemaphoreType.DMA((5,))],
        compiler_params=pltpu.CompilerParams(vmem_limit_bytes=58 * 2**20),
        cost_estimate=pl.CostEstimate(
            flops=2 * m * length * r, bytes_accessed=2 * m * length, transcendentals=0
        ),
        name="first",
    )(models, leaf_in, leaf_up)


def step_kernel(leaf_ref, same_ref):
    same_ref[0] = leaf_ref[0]


def step_call(leaf):
    return pl.pallas_call(
        step_kernel,
        out_shape=jax.ShapeDtypeStruct(leaf.shape, leaf.dtype),
        in_specs=[pl.BlockSpec(memory_space=pltpu.SMEM)],
        out_specs=pl.BlockSpec(memory_space=pltpu.SMEM),
        name="step",
    )(leaf)


def hold_kernel(upper_up_ref, held_ref):
    held_ref[...] = upper_up_ref[...]


def up_kernel(wide_ref, parts_ref, up_ref, sent_ref):
    wide = wide_ref[0]
    own = total_of(parts_ref, 0, parts_ref.shape[0]).astype(BF)
    parent = mm(own, up_ref[0]).astype(BF)
    top = mm(parent, up_ref[1]).astype(BF)
    for k in range(sent_ref.shape[0]):
        sent_ref[k] = top
    for k in range(16):
        sent_ref[wide // 16 * 16 + k] = parent
    for k in range(4):
        sent_ref[wide // 4 * 4 + k] = own


def down_kernel(wide_ref, heard_ref, couple_ref, upper_down, far_ref):
    wide = wide_ref[0]
    nears = []
    for level in range(3):
        step = 4**level
        first = wide // (4 * step) * 4
        near = None
        for s in range(4):
            block = total_of(heard_ref, (first + s) * step, step)
            block = jnp.where(first + s == wide // step, jnp.zeros_like(block), block)
            term = mm(block.astype(BF), couple_ref[level, s])
            near = term if near is None else near + term
        nears.append(near)
    down_ref = upper_down()
    field = nears[2]
    for level in (1, 0):
        field = nears[level] + mm(field.astype(BF), down_ref[level])
    rounded = field.astype(BF)
    for k in range(far_ref.shape[0]):
        far_ref[k] = rounded


def dense_kernel(models_ref, diag_ref, dense_ref):
    dense_ref[...] = mm(models_ref[...], diag_ref[...])


def local_kernel(
    leaf_ref,
    slot_ref,
    next_ref,
    five_ref,
    six_ref,
    two_ref,
    dense_ref,
    couple,
    leaf_down,
    leaf_out,
    base_ref,
    weight_ref,
):
    leaf = leaf_ref[0]
    couple_ref = couple()
    near = mm(next_ref[...], couple_ref[slot_ref[leaf ^ 1]])
    for step, pair_ref in ((5, five_ref), (6, six_ref), (2, two_ref)):
        for k in range(2):
            near = near + mm(pair_ref[k], couple_ref[slot_ref[leaf ^ step ^ k]])
    out = leaf_out()[...]
    base_ref[...] = dense_ref[...] + mm(near.astype(BF), out)
    weight_ref[...] = mm(leaf_down()[...], out).astype(BF)


def last_kernel(far_ref, base_ref, weight_ref, response_ref, held_ref, sems):
    m, r = far_ref.shape[0] * far_ref.shape[1], far_ref.shape[2]
    far = far_ref[...].reshape(m, r)
    pieces = sems.shape[0]
    size = m // pieces
    copies = []
    for k in range(pieces):
        rows = slice(k * size, (k + 1) * size)
        held_ref[rows] = base_ref[rows] + mm(far[rows], weight_ref[...])
        copy = pltpu.make_async_copy(held_ref.at[rows], response_ref.at[rows], sems.at[k])
        copy.start()
        copies.append(copy)
    for copy in copies:
        copy.wait()


def last_call(far, base, weight):
    m, length = base.shape
    return pl.pallas_call(
        last_kernel,
        out_shape=jax.ShapeDtypeStruct(base.shape, F32),
        in_specs=[pl.BlockSpec(memory_space=pltpu.VMEM)] * 3,
        out_specs=pl.BlockSpec(memory_space=pl.ANY),
        scratch_shapes=[pltpu.VMEM(base.shape, F32), pltpu.SemaphoreType.DMA((4,))],
        compiler_params=pltpu.CompilerParams(vmem_limit_bytes=32 * 2**20),
        cost_estimate=pl.CostEstimate(
            flops=2 * m * length * weight.shape[0], bytes_accessed=8 * m * length, transcendentals=0
        ),
        name="last",
    )(far, base, weight)


def shards(
    models,
    leaf_slot,
    diag_blocks,
    leaf_in,
    leaf_out,
    leaf_up,
    leaf_down,
    leaf_couple,
    upper_up,
    upper_down,
    upper_couple,
):
    inputs = models[0, 0]
    m, length = inputs.shape
    r = leaf_in.shape[-1]
    n_leaf = lax.axis_size("leaf")
    n_wide = lax.axis_size("wide")
    cut = m // n_leaf
    wide = lax.axis_index("wide").astype(jnp.int32).reshape(1)
    leaf = lax.axis_index("leaf").astype(jnp.int32).reshape(1)


    def partner(x, step):
        return lax.ppermute(x, "leaf", [(k, k ^ step) for k in range(n_leaf)])

    lifted, skeleton = first_call(inputs, leaf_in[0, 0], leaf_up[0, 0], n_leaf)
    lifted, upper_up, leaf = lax.optimization_barrier((lifted, upper_up, leaf))
    parts = lax.all_to_all(lifted, "leaf", 0, 0, tiled=True)
    leaf, skeleton = lax.optimization_barrier((step_call(leaf), skeleton))
    following = partner(skeleton, 1)
    (ups,) = call(hold_kernel, [(upper_up.shape[1:], BF)], [], [upper_up[0]], name="hold")
    (sent,) = call(
        up_kernel, [((n_wide, cut, r), BF)], [wide], [parts, ups], name="up"
    )
    sent, skeleton, following = lax.optimization_barrier((sent, skeleton, following))
    heard = lax.all_to_all(sent, "wide", 0, 0, tiled=True)
    pair = jnp.stack([skeleton, following])
    two, six, five = [partner(pair, step) for step in (2, 6, 5)]
    (far,) = call(
        down_kernel,
        [((n_leaf, cut, r), BF)],
        [wide],
        [heard, upper_couple[0]],
        [upper_down[0]],
        name="down",
    )
    far = lax.all_to_all(far, "leaf", 0, 0, tiled=True)
    (dense,) = call(
        dense_kernel,
        [((m, length), F32)],
        [],
        [inputs, diag_blocks[0, 0]],
        flops=2 * m * length * length,
        name="dense",
    )
    base, weight = call(
        local_kernel,
        [((m, length), F32), ((r, length), BF)],
        [leaf, leaf_slot[0]],
        [following, five, six, two, dense],
        [leaf_couple[0, 0], leaf_down[0, 0], leaf_out[0, 0]],
        flops=2 * m * length * r,
        name="local",
    )
    response = last_call(far, base, weight)
    return response[None, None]


def solution(mesh):
    placed = (
        P("wide", "leaf", None, None),
        P("wide", None),
        P("wide", "leaf", None, None),
        P("wide", "leaf", None, None),
        P("wide", "leaf", None, None),
        P("wide", "leaf", None, None),
        P("wide", "leaf", None, None),
        P("wide", "leaf", None, None, None),
        P("wide", None, None, None),
        P("wide", None, None, None),
        P("wide", None, None, None, None),
    )
    return jax.shard_map(
        shards, mesh=mesh, in_specs=placed, out_specs=P("wide", "leaf", None, None), check_vma=False
    )
```

```python
import jax
import jax.numpy as jnp
from jax import lax
from jax.experimental import pallas as pl
from jax.experimental.pallas import tpu as pltpu
from jax.sharding import PartitionSpec as P

BF = jnp.bfloat16
F32 = jnp.float32


def mm(a, b):
    return jnp.dot(a, b, preferred_element_type=F32)


def call(body, shapes, scalars, arrays, params=(), flops=10**6, grant=32, name=None):
    n_scalars, n_arrays, n_params, n_out = len(scalars), len(arrays), len(params), len(shapes)

    def kernel(*refs):
        inside = n_scalars + n_arrays
        held = refs[inside + n_params + n_out : inside + 2 * n_params + n_out]
        copies = []
        for k in range(n_params):
            copy = pltpu.make_async_copy(refs[inside + k], held[k], refs[-1].at[k])
            copy.start()
            copies.append(copy)

        def fetch(k):
            def get():
                copies[k].wait()
                return held[k]

            return get

        outs = refs[inside + n_params : inside + n_params + n_out]
        body(*refs[:inside], *[fetch(k) for k in range(n_params)], *outs)

    moved = sum(a.size * a.dtype.itemsize for a in (*arrays, *params))
    return pl.pallas_call(
        kernel,
        out_shape=[jax.ShapeDtypeStruct(s, t) for s, t in shapes],
        in_specs=[pl.BlockSpec(memory_space=pltpu.SMEM)] * n_scalars
        + [pl.BlockSpec(memory_space=pltpu.VMEM)] * n_arrays
        + [pl.BlockSpec(memory_space=pltpu.HBM)] * n_params,
        out_specs=[pl.BlockSpec(memory_space=pltpu.VMEM)] * n_out,
        scratch_shapes=[pltpu.VMEM(a.shape, a.dtype) for a in params]
        + [pltpu.SemaphoreType.DMA((max(n_params, 1),))],
        compiler_params=pltpu.CompilerParams(vmem_limit_bytes=grant * 2**20),
        cost_estimate=pl.CostEstimate(flops=flops, bytes_accessed=moved, transcendentals=0),
        name=name,
    )(*scalars, *arrays, *params)


def total_of(ref, start, count):
    total = ref[start].astype(F32)
    for k in range(1, count):
        total = total + ref[start + k].astype(F32)
    return total


def first_kernel(models_ref, in_ref, up_ref, lifted_ref, skeleton_ref, models, leaf_in, up, sems):
    half = models.shape[1] // 2
    copies = []
    for k in range(2):
        cut = pl.ds(k * half, half)
        copies.append(
            pltpu.make_async_copy(models_ref.at[:, cut], models.at[:, cut], sems.at[2 * k])
        )
        copies.append(pltpu.make_async_copy(in_ref.at[cut], leaf_in.at[cut], sems.at[2 * k + 1]))
    copies.append(pltpu.make_async_copy(up_ref, up, sems.at[4]))
    for copy in copies:
        copy.start()
    coeff = None
    for k in range(2):
        cut = pl.ds(k * half, half)
        copies[2 * k].wait()
        copies[2 * k + 1].wait()
        term = mm(models[:, cut], leaf_in[cut])
        coeff = term if coeff is None else coeff + term
    skeleton = coeff.astype(BF)
    skeleton_ref[...] = skeleton
    copies[4].wait()
    lifted_ref[...] = mm(skeleton, up[...]).astype(BF).reshape(lifted_ref.shape)


def first_call(models, leaf_in, leaf_up, n_leaf):
    m, length = models.shape
    r = leaf_in.shape[1]
    return pl.pallas_call(
        first_kernel,
        out_shape=[
            jax.ShapeDtypeStruct((n_leaf, m // n_leaf, r), BF),
            jax.ShapeDtypeStruct((m, r), BF),
        ],
        in_specs=[pl.BlockSpec(memory_space=pl.ANY)] * 3,
        out_specs=[pl.BlockSpec(memory_space=pltpu.VMEM)] * 2,
        scratch_shapes=[pltpu.VMEM(a.shape, BF) for a in (models, leaf_in, leaf_up)]
        + [pltpu.SemaphoreType.DMA((5,))],
        compiler_params=pltpu.CompilerParams(vmem_limit_bytes=58 * 2**20),
        cost_estimate=pl.CostEstimate(
            flops=2 * m * length * r, bytes_accessed=2 * m * length, transcendentals=0
        ),
        name="first",
    )(models, leaf_in, leaf_up)


def hold_kernel(upper_up_ref, held_ref):
    held_ref[...] = upper_up_ref[...]


def up_kernel(wide_ref, parts_ref, up_ref, sent_ref):
    wide = wide_ref[0]
    own = total_of(parts_ref, 0, parts_ref.shape[0]).astype(BF)
    parent = mm(own, up_ref[0]).astype(BF)
    top = mm(parent, up_ref[1]).astype(BF)
    for k in range(sent_ref.shape[0]):
        sent_ref[k] = top
    for k in range(16):
        sent_ref[wide // 16 * 16 + k] = parent
    for k in range(4):
        sent_ref[wide // 4 * 4 + k] = own


def fold_kernel(couple_ref, upper_down, folded_ref):
    down_ref = upper_down()
    r = down_ref.shape[-1]
    flat = (4 * r, r)
    folded_ref[0] = couple_ref[0]
    top = mm(couple_ref[2].reshape(flat), down_ref[1]).astype(BF)
    folded_ref[2] = mm(top, down_ref[0]).astype(BF).reshape(4, r, r)
    folded_ref[1] = mm(couple_ref[1].reshape(flat), down_ref[0]).astype(BF).reshape(4, r, r)


def down_kernel(wide_ref, heard_ref, folded_ref, far_ref):
    wide = wide_ref[0]
    field = None
    for level in (2, 1, 0):
        step = 4**level
        first = wide // (4 * step) * 4
        for s in range(4):
            block = total_of(heard_ref, (first + s) * step, step)
            block = jnp.where(first + s == wide // step, jnp.zeros_like(block), block)
            term = mm(block.astype(BF), folded_ref[level, s])
            field = term if field is None else field + term
    rounded = field.astype(BF)
    for k in range(far_ref.shape[0]):
        far_ref[k] = rounded


def dense_kernel(models_ref, diag_ref, dense_ref):
    dense_ref[...] = mm(models_ref[...], diag_ref[...])


def local_kernel(
    leaf_ref,
    slot_ref,
    next_ref,
    five_ref,
    six_ref,
    two_ref,
    dense_ref,
    couple,
    leaf_down,
    leaf_out,
    base_ref,
    weight_ref,
):
    leaf = leaf_ref[0]
    couple_ref = couple()
    near = mm(next_ref[...], couple_ref[slot_ref[leaf ^ 1]])
    for step, pair_ref in ((5, five_ref), (6, six_ref), (2, two_ref)):
        for k in range(2):
            near = near + mm(pair_ref[k], couple_ref[slot_ref[leaf ^ step ^ k]])
    out = leaf_out()[...]
    base_ref[...] = dense_ref[...] + mm(near.astype(BF), out)
    weight_ref[...] = mm(leaf_down()[...], out).astype(BF)


def last_kernel(far_ref, base_ref, weight_ref, response_ref, held_ref, sems):
    m, r = far_ref.shape[0] * far_ref.shape[1], far_ref.shape[2]
    far = far_ref[...].reshape(m, r)
    pieces = sems.shape[0]
    size = m // pieces
    copies = []
    for k in range(pieces):
        rows = slice(k * size, (k + 1) * size)
        held_ref[rows] = base_ref[rows] + mm(far[rows], weight_ref[...])
        copy = pltpu.make_async_copy(held_ref.at[rows], response_ref.at[rows], sems.at[k])
        copy.start()
        copies.append(copy)
    for copy in copies:
        copy.wait()


def last_call(far, base, weight):
    m, length = base.shape
    return pl.pallas_call(
        last_kernel,
        out_shape=jax.ShapeDtypeStruct(base.shape, F32),
        in_specs=[pl.BlockSpec(memory_space=pltpu.VMEM)] * 3,
        out_specs=pl.BlockSpec(memory_space=pl.ANY),
        scratch_shapes=[pltpu.VMEM(base.shape, F32), pltpu.SemaphoreType.DMA((4,))],
        compiler_params=pltpu.CompilerParams(vmem_limit_bytes=32 * 2**20),
        cost_estimate=pl.CostEstimate(
            flops=2 * m * length * weight.shape[0], bytes_accessed=8 * m * length, transcendentals=0
        ),
        name="last",
    )(far, base, weight)


def shards(
    models,
    leaf_slot,
    diag_blocks,
    leaf_in,
    leaf_out,
    leaf_up,
    leaf_down,
    leaf_couple,
    upper_up,
    upper_down,
    upper_couple,
):
    inputs = models[0, 0]
    m, length = inputs.shape
    r = leaf_in.shape[-1]
    n_leaf = lax.axis_size("leaf")
    n_wide = lax.axis_size("wide")
    cut = m // n_leaf
    wide = lax.axis_index("wide").astype(jnp.int32).reshape(1)
    leaf = lax.axis_index("leaf").astype(jnp.int32).reshape(1)


    def partner(x, step):
        return lax.ppermute(x, "leaf", [(k, k ^ step) for k in range(n_leaf)])

    lifted, skeleton = first_call(inputs, leaf_in[0, 0], leaf_up[0, 0], n_leaf)
    lifted, upper_up = lax.optimization_barrier((lifted, upper_up))
    parts = lax.all_to_all(lifted, "leaf", 0, 0, tiled=True)
    following = partner(skeleton, 1)
    (ups,) = call(hold_kernel, [(upper_up.shape[1:], BF)], [], [upper_up[0]], name="hold")
    (sent,) = call(
        up_kernel, [((n_wide, cut, r), BF)], [wide], [parts, ups], name="up"
    )
    sent, skeleton, following, upper_down = lax.optimization_barrier(
        (sent, skeleton, following, upper_down)
    )
    heard = lax.all_to_all(sent, "wide", 0, 0, tiled=True)
    pair = jnp.stack([skeleton, following])
    two, six, five = [partner(pair, step) for step in (2, 6, 5)]
    (folded,) = call(
        fold_kernel,
        [(upper_couple.shape[1:], BF)],
        [],
        [upper_couple[0]],
        [upper_down[0]],
        flops=24 * r * r * r,
        name="fold",
    )
    (far,) = call(
        down_kernel, [((n_leaf, cut, r), BF)], [wide], [heard, folded], name="down"
    )
    far = lax.all_to_all(far, "leaf", 0, 0, tiled=True)
    (dense,) = call(
        dense_kernel,
        [((m, length), F32)],
        [],
        [inputs, diag_blocks[0, 0]],
        flops=2 * m * length * length,
        name="dense",
    )
    base, weight = call(
        local_kernel,
        [((m, length), F32), ((r, length), BF)],
        [leaf, leaf_slot[0]],
        [following, five, six, two, dense],
        [leaf_couple[0, 0], leaf_down[0, 0], leaf_out[0, 0]],
        flops=2 * m * length * r,
        name="local",
    )
    response = last_call(far, base, weight)
    return response[None, None]


def solution(mesh):
    placed = (
        P("wide", "leaf", None, None),
        P("wide", None),
        P("wide", "leaf", None, None),
        P("wide", "leaf", None, None),
        P("wide", "leaf", None, None),
        P("wide", "leaf", None, None),
        P("wide", "leaf", None, None),
        P("wide", "leaf", None, None, None),
        P("wide", None, None, None),
        P("wide", None, None, None),
        P("wide", None, None, None, None),
    )
    return jax.shard_map(
        shards, mesh=mesh, in_specs=placed, out_specs=P("wide", "leaf", None, None), check_vma=False
    )
```

```python
import jax
import jax.numpy as jnp
from jax import lax
from jax.experimental import pallas as pl
from jax.experimental.pallas import tpu as pltpu
from jax.sharding import PartitionSpec as P

BF = jnp.bfloat16
F32 = jnp.float32


def mm(a, b):
    return jnp.dot(a, b, preferred_element_type=F32)


def call(body, shapes, scalars, arrays, params=(), flops=10**6, grant=32, name=None):
    n_scalars, n_arrays, n_params, n_out = len(scalars), len(arrays), len(params), len(shapes)

    def kernel(*refs):
        inside = n_scalars + n_arrays
        held = refs[inside + n_params + n_out : inside + 2 * n_params + n_out]
        copies = []
        for k in range(n_params):
            copy = pltpu.make_async_copy(refs[inside + k], held[k], refs[-1].at[k])
            copy.start()
            copies.append(copy)

        def fetch(k):
            def get():
                copies[k].wait()
                return held[k]

            return get

        outs = refs[inside + n_params : inside + n_params + n_out]
        body(*refs[:inside], *[fetch(k) for k in range(n_params)], *outs)

    moved = sum(a.size * a.dtype.itemsize for a in (*arrays, *params))
    return pl.pallas_call(
        kernel,
        out_shape=[jax.ShapeDtypeStruct(s, t) for s, t in shapes],
        in_specs=[pl.BlockSpec(memory_space=pltpu.SMEM)] * n_scalars
        + [pl.BlockSpec(memory_space=pltpu.VMEM)] * n_arrays
        + [pl.BlockSpec(memory_space=pltpu.HBM)] * n_params,
        out_specs=[pl.BlockSpec(memory_space=pltpu.VMEM)] * n_out,
        scratch_shapes=[pltpu.VMEM(a.shape, a.dtype) for a in params]
        + [pltpu.SemaphoreType.DMA((max(n_params, 1),))],
        compiler_params=pltpu.CompilerParams(vmem_limit_bytes=grant * 2**20),
        cost_estimate=pl.CostEstimate(flops=flops, bytes_accessed=moved, transcendentals=0),
        name=name,
    )(*scalars, *arrays, *params)


def total_of(ref, start, count):
    total = ref[start].astype(F32)
    for k in range(1, count):
        total = total + ref[start + k].astype(F32)
    return total


def first_kernel(models_ref, in_ref, up_ref, lifted_ref, skeleton_ref, models, leaf_in, up, sems):
    half = models.shape[1] // 2
    copies = []
    for k in range(2):
        cut = pl.ds(k * half, half)
        copies.append(
            pltpu.make_async_copy(models_ref.at[:, cut], models.at[:, cut], sems.at[2 * k])
        )
        copies.append(pltpu.make_async_copy(in_ref.at[cut], leaf_in.at[cut], sems.at[2 * k + 1]))
    copies.append(pltpu.make_async_copy(up_ref, up, sems.at[4]))
    for copy in copies:
        copy.start()
    coeff = None
    for k in range(2):
        cut = pl.ds(k * half, half)
        copies[2 * k].wait()
        copies[2 * k + 1].wait()
        term = mm(models[:, cut], leaf_in[cut])
        coeff = term if coeff is None else coeff + term
    skeleton = coeff.astype(BF)
    skeleton_ref[...] = skeleton
    copies[4].wait()
    lifted_ref[...] = mm(skeleton, up[...]).astype(BF).reshape(lifted_ref.shape)


def first_call(models, leaf_in, leaf_up, n_leaf):
    m, length = models.shape
    r = leaf_in.shape[1]
    return pl.pallas_call(
        first_kernel,
        out_shape=[
            jax.ShapeDtypeStruct((n_leaf, m // n_leaf, r), BF),
            jax.ShapeDtypeStruct((m, r), BF),
        ],
        in_specs=[pl.BlockSpec(memory_space=pl.ANY)] * 3,
        out_specs=[pl.BlockSpec(memory_space=pltpu.VMEM)] * 2,
        scratch_shapes=[pltpu.VMEM(a.shape, BF) for a in (models, leaf_in, leaf_up)]
        + [pltpu.SemaphoreType.DMA((5,))],
        compiler_params=pltpu.CompilerParams(vmem_limit_bytes=58 * 2**20),
        cost_estimate=pl.CostEstimate(
            flops=2 * m * length * r, bytes_accessed=2 * m * length, transcendentals=0
        ),
        name="first",
    )(models, leaf_in, leaf_up)


def hold_kernel(upper_up_ref, held_ref):
    held_ref[...] = upper_up_ref[...]


def up_kernel(wide_ref, parts_ref, up_ref, sent_ref):
    wide = wide_ref[0]
    own = total_of(parts_ref, 0, parts_ref.shape[0]).astype(BF)
    parent = mm(own, up_ref[0]).astype(BF)
    top = mm(parent, up_ref[1]).astype(BF)
    for k in range(sent_ref.shape[0]):
        sent_ref[k] = top
    for k in range(16):
        sent_ref[wide // 16 * 16 + k] = parent
    for k in range(4):
        sent_ref[wide // 4 * 4 + k] = own


def fold_kernel(upper_couple, upper_down, folded_ref):
    couple_ref, down_ref = upper_couple(), upper_down()
    r = down_ref.shape[-1]
    flat = (4 * r, r)
    folded_ref[0] = couple_ref[0]
    top = mm(couple_ref[2].reshape(flat), down_ref[1]).astype(BF)
    folded_ref[2] = mm(top, down_ref[0]).astype(BF).reshape(4, r, r)
    folded_ref[1] = mm(couple_ref[1].reshape(flat), down_ref[0]).astype(BF).reshape(4, r, r)


def down_kernel(wide_ref, heard_ref, folded_ref, far_ref):
    wide = wide_ref[0]
    field = None
    for level in (2, 1, 0):
        step = 4**level
        first = wide // (4 * step) * 4
        for s in range(4):
            block = total_of(heard_ref, (first + s) * step, step)
            block = jnp.where(first + s == wide // step, jnp.zeros_like(block), block)
            term = mm(block.astype(BF), folded_ref[level, s])
            field = term if field is None else field + term
    rounded = field.astype(BF)
    for k in range(far_ref.shape[0]):
        far_ref[k] = rounded


def dense_kernel(models_ref, diag_ref, dense_ref):
    dense_ref[...] = mm(models_ref[...], diag_ref[...])


def local_kernel(
    leaf_ref,
    slot_ref,
    next_ref,
    five_ref,
    six_ref,
    two_ref,
    dense_ref,
    couple,
    leaf_down,
    leaf_out,
    base_ref,
    weight_ref,
):
    leaf = leaf_ref[0]
    couple_ref = couple()
    near = mm(next_ref[...], couple_ref[slot_ref[leaf ^ 1]])
    for step, pair_ref in ((5, five_ref), (6, six_ref), (2, two_ref)):
        for k in range(2):
            near = near + mm(pair_ref[k], couple_ref[slot_ref[leaf ^ step ^ k]])
    out = leaf_out()[...]
    base_ref[...] = dense_ref[...] + mm(near.astype(BF), out)
    weight_ref[...] = mm(leaf_down()[...], out).astype(BF)


def last_kernel(far_ref, base_ref, weight_ref, response_ref, held_ref, sems):
    m, r = far_ref.shape[0] * far_ref.shape[1], far_ref.shape[2]
    far = far_ref[...].reshape(m, r)
    pieces = sems.shape[0]
    size = m // pieces
    copies = []
    for k in range(pieces):
        rows = slice(k * size, (k + 1) * size)
        held_ref[rows] = base_ref[rows] + mm(far[rows], weight_ref[...])
        copy = pltpu.make_async_copy(held_ref.at[rows], response_ref.at[rows], sems.at[k])
        copy.start()
        copies.append(copy)
    for copy in copies:
        copy.wait()


def last_call(far, base, weight):
    m, length = base.shape
    return pl.pallas_call(
        last_kernel,
        out_shape=jax.ShapeDtypeStruct(base.shape, F32),
        in_specs=[pl.BlockSpec(memory_space=pltpu.VMEM)] * 3,
        out_specs=pl.BlockSpec(memory_space=pl.ANY),
        scratch_shapes=[pltpu.VMEM(base.shape, F32), pltpu.SemaphoreType.DMA((4,))],
        compiler_params=pltpu.CompilerParams(vmem_limit_bytes=32 * 2**20),
        cost_estimate=pl.CostEstimate(
            flops=2 * m * length * weight.shape[0], bytes_accessed=8 * m * length, transcendentals=0
        ),
        name="last",
    )(far, base, weight)


def shards(
    models,
    leaf_slot,
    diag_blocks,
    leaf_in,
    leaf_out,
    leaf_up,
    leaf_down,
    leaf_couple,
    upper_up,
    upper_down,
    upper_couple,
):
    inputs = models[0, 0]
    m, length = inputs.shape
    r = leaf_in.shape[-1]
    n_leaf = lax.axis_size("leaf")
    n_wide = lax.axis_size("wide")
    cut = m // n_leaf
    wide = lax.axis_index("wide").astype(jnp.int32).reshape(1)
    leaf = lax.axis_index("leaf").astype(jnp.int32).reshape(1)


    def partner(x, step):
        return lax.ppermute(x, "leaf", [(k, k ^ step) for k in range(n_leaf)])

    lifted, skeleton = first_call(inputs, leaf_in[0, 0], leaf_up[0, 0], n_leaf)
    lifted, upper_up = lax.optimization_barrier((lifted, upper_up))
    parts = lax.all_to_all(lifted, "leaf", 0, 0, tiled=True)
    following = partner(skeleton, 1)
    (ups,) = call(hold_kernel, [(upper_up.shape[1:], BF)], [], [upper_up[0]], name="hold")
    (sent,) = call(
        up_kernel, [((n_wide, cut, r), BF)], [wide], [parts, ups], name="up"
    )
    sent, skeleton, following, upper_down = lax.optimization_barrier(
        (sent, skeleton, following, upper_down)
    )
    heard = lax.all_to_all(sent, "wide", 0, 0, tiled=True)
    pair = jnp.stack([skeleton, following])
    two, six, five = [partner(pair, step) for step in (2, 6, 5)]
    (folded,) = call(
        fold_kernel,
        [(upper_couple.shape[1:], BF)],
        [],
        [],
        [upper_couple[0], upper_down[0]],
        flops=24 * r * r * r,
        name="fold",
    )
    (far,) = call(
        down_kernel, [((n_leaf, cut, r), BF)], [wide], [heard, folded], name="down"
    )
    far = lax.all_to_all(far, "leaf", 0, 0, tiled=True)
    (dense,) = call(
        dense_kernel,
        [((m, length), F32)],
        [],
        [inputs, diag_blocks[0, 0]],
        flops=2 * m * length * length,
        name="dense",
    )
    base, weight = call(
        local_kernel,
        [((m, length), F32), ((r, length), BF)],
        [leaf, leaf_slot[0]],
        [following, five, six, two, dense],
        [leaf_couple[0, 0], leaf_down[0, 0], leaf_out[0, 0]],
        flops=2 * m * length * r,
        name="local",
    )
    response = last_call(far, base, weight)
    return response[None, None]


def solution(mesh):
    placed = (
        P("wide", "leaf", None, None),
        P("wide", None),
        P("wide", "leaf", None, None),
        P("wide", "leaf", None, None),
        P("wide", "leaf", None, None),
        P("wide", "leaf", None, None),
        P("wide", "leaf", None, None),
        P("wide", "leaf", None, None, None),
        P("wide", None, None, None),
        P("wide", None, None, None),
        P("wide", None, None, None, None),
    )
    return jax.shard_map(
        shards, mesh=mesh, in_specs=placed, out_specs=P("wide", "leaf", None, None), check_vma=False
    )
```
